128 devices in a mesh: row: 8 (over z, x_hi), col: 16 (over x_lo, y, core).
Axes of the slice: x: 4 (x_hi: 2, x_lo: 2; x = x_hi * 2 + x_lo), y: 4, z: 4, core: 2. Of those that a mesh axis runs over, the one named last changes fastest.
Arguments:
- pair: bfloat16 [1024, 1024, 128], P(('row', 'col')), may hold values from -6 to 6
- residue_mask: int32 [1024], replicated, may hold values from 0 to 1, as said below
- ln_gain: float32 [2, 128], replicated, may hold values from 0.5 to 1.5
- ln_shift: float32 [2, 128], replicated, may hold values from -3 to 3
- w_proj: bfloat16 [2, 128, 512], replicated, may hold values from -0.5 to 0.5
- w_bias: bfloat16 [2, 128, 4], replicated, may hold values from -10.606602 to 10.606602
- gate_bias: float32 [2, 128], replicated, may hold values from -4 to 4
- w_out: bfloat16 [2, 128, 128], replicated, may hold values from -0.5 to 0.5
- out_bias: float32 [2, 128], replicated, may hold values from -3 to 3
Outputs:
- starting_update: bfloat16 [256, 1024, 128], P(('row', 'col'))
- ending_update: bfloat16 [256, 1024, 128], P(('row', 'col'))
The draws below stay inside these ranges and needn't reach their ends.
Inputs may be any that keep to these rules, and one draw needn't show every extreme that they name: `residue_mask`: residue 0 is always a real residue.
All inputs are finite; a program needn't handle non-finite values.
Results may differ from the reference program's by a relative error of at most 0.0065.
The reference program's roundings to bfloat16 on the way count: a program that leaves them out, or rounds other values in their place, can miss the bound.
Values may be sent and summed in bfloat16 or wider, within the bound.
A program may use at most 128 MiB of HBM per device.

```python
import jax
import jax.numpy as jnp
from jax import lax

C = 128
HEADS = 4
DH = 32
RD = 8
WD = 2
N = 1024
N_ROW = 8
N_COL = 16


def draw_residue_mask(key, part):
    key = jax.random.fold_in(key, 11)
    levels = jax.random.randint(key, (N,), 0, 20)
    live = (levels < 17).astype(jnp.int32)
    return live.at[0].set(1)


def draw_w_bias(key, part):
    key = jax.random.fold_in(key, 23)
    base = jnp.clip(jax.random.normal(key, (2, C, HEADS), jnp.float32), -4.0, 4.0)
    factor = 1.5
    return (base * (factor / C ** 0.5)).astype(jnp.bfloat16)


def level_of(stream_key, shape, split, least, top_value):
    def one(dim, parts):
        heights = jax.random.uniform(jax.random.fold_in(jax.random.fold_in(stream_key, 6), dim), (parts,), jnp.float32, least / len(split), top_value / len(split))
        return jnp.repeat(jnp.exp(heights), shape[dim] // parts).reshape((-1,) + (1,) * (len(shape) - dim - 1))

    level = one(*split[0])
    for cut in split[1:]:
        level = level * one(*cut)
    return level


def normal_values(stream_key, extent, deviation, bound, pieces=(), held_as=jnp.bfloat16):
    loudness = level_of(stream_key, extent, pieces, -0.22, 0.18) if pieces else 1.0
    entries = jax.random.normal(stream_key, extent, jnp.float32) * deviation * loudness
    return jnp.minimum(jnp.maximum(entries, -bound), bound).astype(held_as)


def setup_inputs(seed: int = 0) -> dict:
    keys = jax.random.split(jax.random.key(seed), 10)
    return {
        "pair": normal_values(keys[0], (N, N, C), 1.0, 6.0, ((0, 128),)),
        "residue_mask": draw_residue_mask(jax.random.fold_in(keys[9], 71), 0),
        "ln_gain": jnp.clip(1.0 + 0.1 * jax.random.normal(keys[2], (2, C), jnp.float32), 0.5, 1.5),
        "ln_shift": normal_values(keys[3], (2, C), 0.5, 3.0, (), jnp.float32),
        "w_proj": normal_values(keys[4], (2, C, 4 * HEADS * DH), C ** -0.5, 0.5),
        "w_bias": draw_w_bias(jax.random.fold_in(keys[9], 71), 0),
        "gate_bias": normal_values(keys[6], (2, HEADS * DH), 1.0, 4.0, (), jnp.float32),
        "w_out": normal_values(keys[7], (2, HEADS * DH, C), (HEADS * DH) ** -0.5, 0.5),
        "out_bias": normal_values(keys[8], (2, C), 0.5, 3.0, (), jnp.float32),
    }


EPS = 1e-05

def layer_norm(values, gain, shift):
    wide = values.astype(jnp.float32)
    center = lax.optimization_barrier(jnp.mean(wide, -1, keepdims=True))
    spread = lax.optimization_barrier(jnp.mean(jnp.square(wide - center), -1, keepdims=True))
    return ((wide - center) * lax.rsqrt(spread + EPS) * gain + shift).astype(jnp.bfloat16)

def project(normed, weight, offset, head_count):
    lead = normed.shape[:-1]
    inner = weight.shape[1] // 4
    size = inner // head_count
    full = jnp.dot(normed.reshape(-1, normed.shape[-1]), weight, preferred_element_type=jnp.float32)
    queries = (full[:, :inner] * size ** (-0.5)).astype(jnp.bfloat16).reshape(lead + (head_count, size))
    key_rows = full[:, inner:2 * inner].astype(jnp.bfloat16).reshape(lead + (head_count, size))
    value_rows = full[:, 2 * inner:3 * inner].astype(jnp.bfloat16).reshape(lead + (head_count, size))
    gating = jax.nn.sigmoid(full[:, 3 * inner:] + offset).reshape(lead + (inner,))
    return (queries, key_rows, value_rows, gating)

def attend(queries, key_rows, value_rows, gating, bias, live, weight_out, offset_out):
    scores = jnp.einsum('qhd,khd->hqk', queries.astype(jnp.float32), key_rows.astype(jnp.float32)) + bias.astype(jnp.float32)
    scores = jnp.where(live[None, None, :] > 0, scores, jnp.float32(-1000000000.0))
    top = lax.optimization_barrier(jnp.max(scores, -1, keepdims=True))
    expo = jnp.exp(scores - top)
    weights = (expo / lax.optimization_barrier(jnp.sum(expo, -1, keepdims=True))).astype(jnp.bfloat16)
    mixed = jnp.einsum('hqk,khd->qhd', weights.astype(jnp.float32), value_rows.astype(jnp.float32))
    gated = (mixed.reshape(mixed.shape[0], -1) * gating).astype(jnp.bfloat16)
    return (jnp.dot(gated, weight_out, preferred_element_type=jnp.float32) + offset_out).astype(jnp.bfloat16)

def bias_rows(pair, gain, shift, weight):

    def one_line(line):
        normed = layer_norm(line, gain, shift)
        return jnp.dot(normed, weight, preferred_element_type=jnp.float32).astype(jnp.bfloat16)
    return jnp.transpose(lax.map(one_line, pair), (2, 0, 1))

def reference(pair, residue_mask, ln_gain, ln_shift, w_proj, w_bias, gate_bias, w_out, out_bias):
    devices = N_ROW * N_COL
    window_index = (jnp.arange(devices, dtype=jnp.int32)[:, None] * RD + jnp.arange(WD, dtype=jnp.int32)[None, :]).reshape(-1).astype(jnp.int32)
    start_bias = bias_rows(pair, ln_gain[0], ln_shift[0], w_bias[0])
    end_bias = jnp.transpose(bias_rows(pair, ln_gain[1], ln_shift[1], w_bias[1]), (0, 2, 1))

    def run(line, which, bias):
        normed = layer_norm(line, ln_gain[which], ln_shift[which])
        queries, key_rows, value_rows, gating = project(normed, w_proj[which], gate_bias[which], HEADS)
        return attend(queries, key_rows, value_rows, gating, bias, residue_mask, w_out[which], out_bias[which])
    starting_update = lax.map(lambda index: run(pair[index], 0, start_bias), window_index)
    ending_update = lax.map(lambda index: run(pair[:, index, :], 1, end_bias), window_index)
    return (starting_update, ending_update)
```

```python
import jax
import jax.numpy as jnp
from jax import lax
from jax.experimental import pallas as pl
from jax.experimental.pallas import tpu as pltpu
from jax.sharding import PartitionSpec as P

N, C, HEADS, DH, RD = 1024, 128, 4, 32, 8
BF, F32 = jnp.bfloat16, jnp.float32
MESH = pl.DeviceIdType.MESH
NT = (((1,), (1,)), ((), ()))
NEG = -1e30
EPS = 1e-05
ORDERS = ((2, 1, 0), (0, 2, 1), (1, 0, 2))
PICKED = (0, 1, 8, 9)


def tile_at(h, lt):
    if isinstance(h, int) and isinstance(lt, int):
        return (lt // 3 + h) % 3 * 12 + h * 3 + lt % 3
    return lax.rem(lt // 3 + h, 3) * 12 + h * 3 + lax.rem(lt, 3)


def device_of(z, x, y, core):
    return (z * 2 + x // 2, lax.rem(x, 2) * 8 + y * 2 + core)


def stats_norm(x):
    center = jnp.mean(x, -1, keepdims=True)
    d = x - center
    spread = jnp.mean(d * d, -1, keepdims=True)
    return d * lax.rsqrt(spread + EPS)


def norm(x, gain, shift):
    return (stats_norm(x) * gain + shift).astype(BF)


def body(
    pair, mask, gain, shift, w_proj, w_bias, gate_bias, w_out, out_bias,
    out0, out1,
    G, xf, pkf, pk, cols, rowsbuf, bacc, xb,
    wq, wo, gb, wkt, lnorm, qr, kp, kpt, vp, gate, acc, sA, sB, mA, mB, ost,
    ag_s, ag_r, aa_s, aa_r, ms_s, ms_r,
):
    row, col = lax.axis_index("row"), lax.axis_index("col")
    me = row * 16 + col
    z, x = row // 2, lax.rem(row, 2) * 2 + col // 8
    y, core = lax.rem(col // 2, 4), lax.rem(col, 2)
    pos = (z, x, y)
    partner = (row, col + 1 - 2 * core)
    barrier = pltpu.get_barrier_semaphore()

    def signal(dev):
        pl.semaphore_signal(barrier, inc=1, device_id=dev, device_id_type=MESH)

    def beside(axis, by):
        p = list(pos)
        p[axis] = lax.rem(p[axis] + by, 4)
        return device_of(*p, core)

    @pl.when(core == 0)
    def _():
        signal(partner)
        for axis in range(3):
            signal(beside(axis, 1))
            signal(beside(axis, 3))

    @pl.when(core == 1)
    def _():
        def one(d, _):
            @pl.when(d != me)
            def _():
                signal((d // 16, lax.rem(d, 16)))

            return 0

        lax.fori_loop(0, 128, one, 0)

    def pick(a, _):
        xf[...] = pair[a].astype(F32)
        for q in range(4):
            pkf[pl.ds(q * 8 + a, 64, stride=32), :] = xf[pl.ds(PICKED[q], 64, stride=16), :]
        return 0

    lax.fori_loop(0, RD, pick, 0)

    def pack(i, _):
        pk[pl.ds(i * 8, 8)] = pkf[pl.ds(pl.multiple_of(i * 256, 256), 256), :].reshape(8, 32, 128).astype(BF)
        return 0

    lax.fori_loop(0, 8, pack, 0)

    pl.semaphore_wait(barrier, 70 - 6 * core)

    def to_chip(c, _):
        @pl.when(2 * c + 1 != me)
        def _():
            pltpu.make_async_remote_copy(
                pk.at[c], cols.at[me], aa_s, aa_r, device_id=(c // 8, lax.rem(c, 8) * 2 + 1), device_id_type=MESH
            ).start()

        return 0

    lax.fori_loop(0, 64, to_chip, 0)

    rows_copy = pltpu.make_async_remote_copy(
        pair.at[pl.ds(0, 2)], rowsbuf, ms_s.at[0], ms_r.at[0], device_id=partner, device_id_type=MESH
    )

    @pl.when(core == 1)
    def _():
        rows_copy.start()
        cols[me] = pk[me // 2]

    wcat = []
    for p in range(2):
        w = jnp.concatenate([w_bias[p].astype(F32), jnp.zeros((128, 124), F32)], 1)
        wcat.append(jnp.transpose(w))
    zero8 = jnp.zeros((8, 128), F32)
    wrep = jnp.concatenate(
        [
            jnp.concatenate(
                [jnp.broadcast_to(wcat[p][h : h + 1], (8, 128)) if s == p else zero8 for s in range(2)], 1
            )
            for p in range(2)
            for h in range(4)
        ],
        0,
    )
    r8 = lax.rem(lax.broadcasted_iota(jnp.int32, (64, 256), 0), 8)

    def bias_row(a, _):
        lhs = jnp.where(r8 == a, wrep, 0.0).astype(BF)
        for b in range(4):
            xn = stats_norm(pair[a, b * 256 : (b + 1) * 256, :].astype(F32))
            both = jnp.concatenate([(xn * gain[p : p + 1] + shift[p : p + 1]).astype(BF) for p in range(2)], 1)
            part = lax.dot_general(lhs, both, NT, preferred_element_type=F32)
            s = slice(b * 256, (b + 1) * 256)
            bacc[:, s] = jnp.where(a == 0, 0.0, bacc[:, s]) + part
        return 0

    bacc[...] = jnp.zeros((64, N), F32)
    lax.fori_loop(0, RD, bias_row, 0)
    live = jnp.broadcast_to(mask[...], (8, N))
    lane8 = lax.broadcasted_iota(jnp.int32, (8, N), 1)
    sub8 = lax.broadcasted_iota(jnp.int32, (8, N), 0)
    own = jnp.sum(jnp.where(lane8 == me * 8 + sub8, live, 0), -1, keepdims=True)
    own = jnp.broadcast_to(own, (8, N))
    for ph in range(8):
        keep = (live if ph < 4 else own) > 0
        bacc[ph * 8 : ph * 8 + 8, :] = jnp.where(keep, bacc[ph * 8 : ph * 8 + 8, :], NEG)
    half_copy = pltpu.make_async_remote_copy(
        bacc.at[pl.ds(pl.multiple_of((1 - core) * 32, 32), 32)],
        xb, ms_s.at[1], ms_r.at[1], device_id=partner, device_id_type=MESH,
    )
    half_copy.start()

    def prep_weights():
        for q in range(4):
            for blk in range(4):
                w = w_proj[core, :, blk * 128 : (blk + 1) * 128].astype(F32)
                if q:
                    w = pltpu.roll(w, 32 * q, 1)
                wq[q, :, blk * 128 : (blk + 1) * 128] = w.astype(BF)
                if blk == 1:
                    wkt[q] = jnp.transpose(w).astype(BF)
            o = w_out[core].astype(F32)
            g = jnp.broadcast_to(gate_bias[pl.ds(core, 1)], (8, 128))
            if q:
                o = pltpu.roll(o, 32 * q, 0)
                g = pltpu.roll(g, 32 * q, 1)
            wo[q] = o.astype(BF)
            gb[q] = g
        vp[:, :, 128:] = jnp.ones((4, N, 128), BF)
        acc[...] = jnp.zeros_like(acc)

    prep_weights()

    half_copy.wait_recv()
    mine = pl.multiple_of(core * 32, 32)
    for h in range(4):
        ours = bacc[pl.ds(pl.multiple_of(mine + h * 8, 8), 8), :]
        theirs = xb[h * 8 : h * 8 + 8, :]
        low = jnp.where(core == 0, ours, theirs)
        high = jnp.where(core == 0, theirs, ours)
        block = jnp.concatenate([low, high], 0).astype(BF)
        for lt in range(8):
            G[z, x, y, tile_at(h, lt)] = block[:, lt * 128 : (lt + 1) * 128]
    for r in range(3):
        for h in range(4):
            if (r - h) % 3 == 2:
                G[z, x, y, r * 12 + h * 3 + 2] = jnp.zeros((16, 128), BF)

    def region(axis, at, free, tiles, half=None):
        index = list(pos)
        for f in free:
            index[f] = pl.ds(0, 4)
        if half is not None and free:
            index[free[0]] = pl.ds(2 * half, 2)
        if half is not None and not free:
            tiles = (tiles[0] + half * (tiles[1] // 2), tiles[1] // 2)
        index[axis] = at
        return G.at[index[0], index[1], index[2], pl.ds(tiles[0], tiles[1])]

    def ring(r, phase, h):
        axis, free = ORDERS[r][phase], ORDERS[r][:phase]
        if phase < 2:
            tiles, sem = (r * 12, 12), phase * 12 + r * 4
        else:
            tiles, sem = (r * 12 + h * 3, 2 if (r - h) % 3 == 2 else 3), 24 + h * 12 + r * 4
        v = pos[axis]
        up, down, far = lax.rem(v + 1, 4), lax.rem(v + 3, 4), lax.rem(v + 2, 4)

        def copy(at, half, k, to):
            ref = region(axis, at, free, tiles, half)
            return pltpu.make_async_remote_copy(
                ref, ref, ag_s.at[sem + k], ag_r.at[sem + k], device_id=beside(axis, to), device_id_type=MESH
            )

        sends = ((v, None, 0, 1), (v, None, 1, 3), (down, 0, 2, 1), (up, 1, 3, 3))
        gets = ((down, None, 0, 1), (up, None, 1, 3), (far, 0, 2, 1), (far, 1, 3, 3))
        return (lambda k: copy(*sends[k])), (lambda k: copy(*gets[k]))

    def start(phase, step, h=0):
        for r in range(3):
            sends, _ = ring(r, phase, h)
            for k in (2 * step, 2 * step + 1):
                sends(k).start()

    def arrive(phase, step, h=0):
        for r in range(3):
            _, gets = ring(r, phase, h)
            for k in (2 * step, 2 * step + 1):
                gets(k).wait_recv()

    def line(q):
        g, s = gain[pl.ds(core, 1)], shift[pl.ds(core, 1)]
        R = 256

        @pl.when(core == 0)
        def _():
            def step(i, _):
                rr = pl.ds(pl.multiple_of(i * R, R), R)
                src = pair[q, rr, :] if q < 2 else rowsbuf[q - 2, rr, :]
                lnorm[rr, :] = norm(src.astype(F32), g, s)
                return 0

            lax.fori_loop(0, N // R, step, 0)

        @pl.when(core == 1)
        def _():
            def step(i, _):
                rr = pl.ds(pl.multiple_of(i * R, R), R)
                v = cols[pl.ds(i * (R // 8), R // 8), q // 2 * 16 : q // 2 * 16 + 16, :].astype(F32)
                lnorm[rr, :] = norm(v[:, q % 2 * 8 : q % 2 * 8 + 8, :].reshape(R, 128), g, s)
                return 0

            lax.fori_loop(0, N // R, step, 0)

        def step(i, _):
            rr = pl.ds(pl.multiple_of(i * R, R), R)
            full = jnp.dot(lnorm[rr, :], wq[q], preferred_element_type=F32)
            qr[q, rr, :] = (full[:, :128] * DH**-0.5).astype(BF)
            k = full[:, 128:256].astype(BF)
            v = full[:, 256:384].astype(BF)
            for h in range(4):
                sl = slice(32 * ((q + h) % 4), 32 * ((q + h) % 4) + 32)
                kp[h, rr, sl] = k[:, sl]
                vp[h, rr, sl] = v[:, sl]
            gate[q, rr, :] = jax.nn.sigmoid(full[:, 384:] + gb[q, 0:1])
            return 0

        lax.fori_loop(0, N // R, step, 0)

        @pl.when(core == 0)
        def _():
            kt = lax.dot_general(wkt[q], lnorm[...], NT, preferred_element_type=F32).astype(BF)
            for h in range(4):
                s = (q + h) % 4
                kpt[h, 32 * s : 32 * s + 32, :] = kt[32 * s : 32 * s + 32, :]

    start(0, 0)

    @pl.when(core == 0)
    def _():
        rows_copy.wait_recv()

    @pl.when(core == 1)
    def _():
        rows_copy.wait_send()
        every = cols.at[pl.ds(0, 127)]
        pltpu.make_async_remote_copy(
            every, every, aa_s, aa_r, device_id=partner, device_id_type=MESH
        ).wait_recv()

    line(0)
    arrive(0, 0)
    start(0, 1)
    line(1)
    arrive(0, 1)
    start(1, 0)
    line(2)
    arrive(1, 0)
    start(1, 1)
    line(3)
    arrive(1, 1)
    start(2, 0, 0)
    start(2, 0, 1)
    arrive(2, 0, 0)
    start(2, 1, 0)
    start(2, 0, 2)
    arrive(2, 1, 0)

    lane = lax.broadcasted_iota(jnp.int32, (128, 128), 1)
    sub = lax.broadcasted_iota(jnp.int32, (128, 128), 0)
    slot = lane // 32

    def scores(c, h, jb, S, M):
        rows = pl.ds(pl.multiple_of(jb * 128, 128), 128)
        eye = (lane == sub).astype(F32).astype(BF)
        lhs = []
        for q in range(4):
            m = (slot == lax.rem(q + h, 4)).astype(F32).astype(BF)
            lhs.append(jnp.concatenate([qr[q, rows, :] * m, eye], 1))
        lhs = jnp.concatenate(lhs, 0)
        top = None
        for n in range(4):
            if c == 0:
                b = jnp.concatenate(
                    [
                        G[jb // 2, pl.ds(lax.rem(jb, 2) * 2, 2), :, tile_at(h, lt)].reshape(128, 128)
                        for lt in (2 * n, 2 * n + 1)
                    ],
                    1,
                )
                rhs = jnp.concatenate([kpt[h, :, n * 256 : (n + 1) * 256], b], 0)
                s = jnp.dot(lhs, rhs, preferred_element_type=F32)
            else:
                b = G[n, :, :, tile_at(h, jb)].reshape(256, 128)
                rhs = jnp.concatenate([kp[h, n * 256 : (n + 1) * 256, :], b], 1)
                s = lax.dot_general(lhs, rhs, NT, preferred_element_type=F32)
            S[:, n * 256 : (n + 1) * 256] = s
            t = jnp.maximum(s[:, :128], s[:, 128:])
            top = t if top is None else jnp.maximum(top, t)
        M[...] = jnp.broadcast_to(jnp.max(top, -1, keepdims=True), (512, 128))

    def mix(h, jb, S, M):
        rows = pl.ds(pl.multiple_of(jb * 128, 128), 128)
        p = jnp.exp(S[...] - jnp.concatenate([M[...]] * 8, 1)).astype(BF)
        o = jnp.dot(p, vp[h], preferred_element_type=F32)
        for q in range(4):
            oq = o[q * 128 : (q + 1) * 128]
            val = oq[:, :128] / oq[:, 128:] * gate[q, rows, :]
            acc[q, rows, :] = jnp.where(slot == lax.rem(q + h, 4), val, acc[q, rows, :])

    for c in range(2):
        pl.when(core == c)(lambda c=c: scores(c, 0, 0, sA, mA))

    def pair_of_units(i, _):
        @pl.when(i == 1)
        def _():
            arrive(2, 0, 1)
            start(2, 1, 1)
            start(2, 0, 3)

        @pl.when(i == 3)
        def _():
            arrive(2, 1, 1)

        @pl.when(i == 5)
        def _():
            arrive(2, 0, 2)
            start(2, 1, 2)

        @pl.when(i == 7)
        def _():
            arrive(2, 1, 2)

        @pl.when(i == 9)
        def _():
            arrive(2, 0, 3)
            start(2, 1, 3)

        @pl.when(i == 11)
        def _():
            arrive(2, 1, 3)

        u0 = 2 * i
        u1 = u0 + 1
        u2 = lax.rem(u0 + 2, 32)
        for c in range(2):

            @pl.when(core == c)
            def _(c=c):
                scores(c, u1 // 8, lax.rem(u1, 8), sB, mB)
                mix(u0 // 8, lax.rem(u0, 8), sA, mA)
                scores(c, u2 // 8, lax.rem(u2, 8), sA, mA)
                mix(u1 // 8, lax.rem(u1, 8), sB, mB)

        return 0

    lax.fori_loop(0, 16, pair_of_units, 0)

    def finish(jb, _):
        rows = pl.ds(pl.multiple_of(jb * 128, 128), 128)
        for q in range(4):
            o = jnp.dot(acc[q, rows, :].astype(BF), wo[q], preferred_element_type=F32)
            ost[q, rows, :] = (o + out_bias[pl.ds(core, 1)]).astype(BF)
        return 0

    lax.fori_loop(0, 8, finish, 0)

    for c, out in ((0, out0), (1, out1)):

        @pl.when(core == c)
        def _(c=c, out=out):
            away = pltpu.make_async_remote_copy(
                ost.at[pl.ds(2 - 2 * c, 2)], out, ms_s.at[2 + c], ms_r.at[2 + c], device_id=partner, device_id_type=MESH
            )
            away.start()
            home = pltpu.make_async_copy(ost.at[pl.ds(2 * c, 2)], out, ms_s.at[4])
            home.start()
            home.wait()
            away.wait_send()

    for c, out in ((1, out0), (0, out1)):

        @pl.when(core == c)
        def _(c=c, out=out):
            pltpu.make_async_remote_copy(
                ost.at[pl.ds(0, 2)], out, ms_s.at[3 - c], ms_r.at[3 - c], device_id=partner, device_id_type=MESH
            ).wait_recv()

    half_copy.wait_send()

    @pl.when(core == 0)
    def _():
        pltpu.make_async_remote_copy(pk, pk, aa_s, aa_r, device_id=partner, device_id_type=MESH).wait_send()

    @pl.when(core == 1)
    def _():
        most = pk.at[pl.ds(0, 63)]
        pltpu.make_async_remote_copy(most, most, aa_s, aa_r, device_id=partner, device_id_type=MESH).wait_send()

    for phase, heads in ((0, (0,)), (1, (0,)), (2, range(4))):
        for h in heads:
            for r in range(3):
                for k in range(4):
                    ring(r, phase, h)[0](k).wait_send()


def local(pair, residue_mask, ln_gain, ln_shift, w_proj, w_bias, gate_bias, w_out, out_bias):
    vmem = pl.BlockSpec(memory_space=pltpu.VMEM)
    out = jax.ShapeDtypeStruct((2, N, C), BF)
    V = pltpu.VMEM
    dma = pltpu.SemaphoreType.DMA
    return pl.pallas_call(
        body,
        out_shape=(out, out),
        in_specs=[vmem] * 9,
        out_specs=(pl.BlockSpec(memory_space=pl.ANY),) * 2,
        scratch_shapes=[
            V((4, 4, 4, 36, 16, 128), BF), V((N, C), F32), V((2048, C), F32), V((64, 32, C), BF), V((128, 32, C), BF),
            V((2, N, C), BF), V((64, N), F32), V((32, N), F32),
            V((4, 128, 512), BF), V((4, 128, 128), BF), V((4, 8, 128), F32), V((4, 128, 128), BF), V((N, C), BF),
            V((4, N, C), BF), V((4, N, C), BF), V((4, C, N), BF), V((4, N, 256), BF), V((4, N, C), F32), V((4, N, C), F32),
            V((512, N), F32), V((512, N), F32), V((512, 128), F32), V((512, 128), F32), V((4, N, C), BF),
            dma((72,)), dma((72,)), dma, dma, dma((5,)), dma((4,)),
        ],
        compiler_params=pltpu.CompilerParams(
            collective_id=0, has_side_effects=True, vmem_limit_bytes=56 * 2**20
        ),
        cost_estimate=pl.CostEstimate(flops=20 * 10**9, bytes_accessed=4 * 2**20, transcendentals=17 * 10**6),
    )(pair, residue_mask.reshape(1, N), ln_gain, ln_shift, w_proj, w_bias, gate_bias, w_out, out_bias)


def solution(mesh):
    return jax.shard_map(
        local,
        mesh=mesh,
        in_specs=(P(("row", "col"), None, None), P(), P(), P(), P(), P(), P(), P(), P()),
        out_specs=(P(("row", "col"), None, None), P(("row", "col"), None, None)),
        check_vma=False,
    )
```

```python
import jax
import jax.numpy as jnp
from jax import lax
from jax.experimental import pallas as pl
from jax.experimental.pallas import tpu as pltpu
from jax.sharding import PartitionSpec as P

N, C, HEADS, DH, RD = 1024, 128, 4, 32, 8
BF, F32 = jnp.bfloat16, jnp.float32
MESH = pl.DeviceIdType.MESH
NT = (((1,), (1,)), ((), ()))
NEG = -1e30
EPS = 1e-05
ORDERS = ((2, 1, 0), (0, 2, 1), (1, 0, 2))
PICKED = (0, 1, 8, 9)


def tile_at(h, lt):
    if isinstance(h, int) and isinstance(lt, int):
        return (lt // 3 + h) % 3 * 12 + h * 3 + lt % 3
    return lax.rem(lt // 3 + h, 3) * 12 + h * 3 + lax.rem(lt, 3)


def device_of(z, x, y, core):
    return (z * 2 + x // 2, lax.rem(x, 2) * 8 + y * 2 + core)


def stats_norm(x):
    center = jnp.mean(x, -1, keepdims=True)
    d = x - center
    spread = jnp.mean(d * d, -1, keepdims=True)
    return d * lax.rsqrt(spread + EPS)


def norm(x, gain, shift):
    return (stats_norm(x) * gain + shift).astype(BF)


def body(
    pair_hbm, mask, gain, shift, w_proj, w_bias, gate_bias, w_out, out_bias,
    out0, out1,
    G, pair, xf, pkf, pk, cols, rowsbuf, bacc, xb,
    wq, wo, gb, wkt, lnorm, qr, kp, kpt, vp, gate, acc, sA, sB, mA, mB, ost,
    ag_s, ag_r, aa_s, aa_r, ms_s, ms_r, ld_s,
):
    row, col = lax.axis_index("row"), lax.axis_index("col")
    me = row * 16 + col
    z, x = row // 2, lax.rem(row, 2) * 2 + col // 8
    y, core = lax.rem(col // 2, 4), lax.rem(col, 2)
    pos = (z, x, y)
    partner = (row, col + 1 - 2 * core)
    barrier = pltpu.get_barrier_semaphore()

    def signal(dev):
        pl.semaphore_signal(barrier, inc=1, device_id=dev, device_id_type=MESH)

    def beside(axis, by):
        p = list(pos)
        p[axis] = lax.rem(p[axis] + by, 4)
        return device_of(*p, core)

    def load(a):
        return pltpu.make_async_copy(pair_hbm.at[a], pair.at[a], ld_s.at[a])

    for a in range(RD):
        load(a).start()

    @pl.when(core == 0)
    def _():
        signal(partner)
        for axis in range(3):
            for by in (1, 2, 3):
                signal(beside(axis, by))

    @pl.when(core == 1)
    def _():
        def one(i, _):
            d = lax.rem(me + i, 128)
            signal((d // 16, lax.rem(d, 16)))
            return 0

        lax.fori_loop(1, 128, one, 0)

    def pick(a):
        load(a).wait()
        xf[...] = pair[a].astype(F32)
        for q in range(4):
            pkf[pl.ds(q * 8 + a, 64, stride=32), :] = xf[pl.ds(PICKED[q], 64, stride=16), :]

    for a in range(RD):
        pick(a)

    def pack(i, _):
        pk[pl.ds(i * 8, 8)] = pkf[pl.ds(pl.multiple_of(i * 256, 256), 256), :].reshape(8, 32, 128).astype(BF)
        return 0

    lax.fori_loop(0, 8, pack, 0)

    def remote(src, dst, send, recv, dev):
        return pltpu.make_async_remote_copy(src, dst, send, recv, device_id=dev, device_id_type=MESH)

    def plus(v, k):
        return lax.rem(v + k, 4)

    def picked_send():
        chip = me // 2

        def one(i, _):
            c = lax.rem(chip + i, 64)
            remote(pk.at[c], cols.at[me], aa_s, aa_r, (c // 8, lax.rem(c, 8) * 2 + 1)).start()
            return 0

        lax.fori_loop(1, 64, one, 0)

        @pl.when(core == 0)
        def _():
            remote(pk.at[chip], cols.at[me], aa_s, aa_r, partner).start()

        @pl.when(core == 1)
        def _():
            cols[me] = pk[chip]

    def picked_end():
        @pl.when(core == 1)
        def _():
            every = cols.at[pl.ds(0, 127)]
            remote(every, every, aa_s, aa_r, partner).wait_recv()

    rows_copy = remote(pair.at[pl.ds(0, 2)], rowsbuf, ms_s.at[0], ms_r.at[0], partner)

    wcat = []
    for p in range(2):
        wcat.append(w_bias[p].astype(F32))
    zero8 = jnp.zeros((8, 128), F32)
    wrep = jnp.concatenate(
        [
            jnp.concatenate(
                [jnp.broadcast_to(wcat[p][h : h + 1], (8, 128)) if s == p else zero8 for s in range(2)], 1
            )
            for p in range(2)
            for h in range(4)
        ],
        0,
    )
    r8 = lax.rem(lax.broadcasted_iota(jnp.int32, (64, 256), 0), 8)

    def bias_row(a, _):
        lhs = jnp.where(r8 == a, wrep, 0.0).astype(BF)
        for b in range(4):
            xn = stats_norm(pair[a, b * 256 : (b + 1) * 256, :].astype(F32))
            both = jnp.concatenate([(xn * gain[p : p + 1] + shift[p : p + 1]).astype(BF) for p in range(2)], 1)
            part = lax.dot_general(lhs, both, NT, preferred_element_type=F32)
            s = slice(b * 256, (b + 1) * 256)
            bacc[:, s] = jnp.where(a == 0, 0.0, bacc[:, s]) + part
        return 0

    bacc[...] = jnp.zeros((64, N), F32)
    lax.fori_loop(0, RD, bias_row, 0)
    live = jnp.broadcast_to(mask[...], (8, N))
    lane8 = lax.broadcasted_iota(jnp.int32, (8, N), 1)
    sub8 = lax.broadcasted_iota(jnp.int32, (8, N), 0)
    own = jnp.sum(jnp.where(lane8 == me * 8 + sub8, live, 0), -1, keepdims=True)
    own = jnp.broadcast_to(own, (8, N))
    for ph in range(8):
        keep = (live if ph < 4 else own) > 0
        bacc[ph * 8 : ph * 8 + 8, :] = jnp.where(keep, bacc[ph * 8 : ph * 8 + 8, :], NEG)
    half_copy = pltpu.make_async_remote_copy(
        bacc.at[pl.ds(pl.multiple_of((1 - core) * 32, 32), 32)],
        xb, ms_s.at[1], ms_r.at[1], device_id=partner, device_id_type=MESH,
    )
    pl.semaphore_wait(barrier, 73 - 9 * core)
    half_copy.start()

    @pl.when(core == 1)
    def _():
        rows_copy.start()

    def prep_weights():
        for q in range(4):
            for blk in range(4):
                w = w_proj[core, :, blk * 128 : (blk + 1) * 128].astype(F32)
                if q:
                    w = pltpu.roll(w, 32 * q, 1)
                wq[q, :, blk * 128 : (blk + 1) * 128] = w.astype(BF)
                if blk == 1:
                    wkt[q] = jnp.transpose(w).astype(BF)
            o = w_out[core].astype(F32)
            g = jnp.broadcast_to(gate_bias[pl.ds(core, 1)], (8, 128))
            if q:
                o = pltpu.roll(o, 32 * q, 0)
                g = pltpu.roll(g, 32 * q, 1)
            wo[q] = o.astype(BF)
            gb[q] = g
        vp[:, :, 128:] = jnp.ones((4, N, 128), BF)
        acc[...] = jnp.zeros_like(acc)

    prep_weights()

    half_copy.wait_recv()
    mine = pl.multiple_of(core * 32, 32)
    for h in range(4):
        ours = bacc[pl.ds(pl.multiple_of(mine + h * 8, 8), 8), :]
        theirs = xb[h * 8 : h * 8 + 8, :]
        low = jnp.where(core == 0, ours, theirs)
        high = jnp.where(core == 0, theirs, ours)
        block = jnp.concatenate([low, high], 0).astype(BF)
        for lt in range(8):
            G[z, x, y, tile_at(h, lt)] = block[:, lt * 128 : (lt + 1) * 128]
    for r in range(3):
        for h in range(4):
            if (r - h) % 3 == 2:
                G[z, x, y, r * 12 + h * 3 + 2] = jnp.zeros((16, 128), BF)

    names = {}

    def sem(*name):
        return names.setdefault(name, len(names))

    def region(r, tiles, u, v, w):
        index = [0, 0, 0]
        for axis, at in zip(ORDERS[r], (u, v, w)):
            index[axis] = at
        return G.at[index[0], index[1], index[2], tiles]

    def gather_copy(ref, name, axis, by):
        return remote(ref, ref, ag_s.at[sem(*name)], ag_r.at[sem(*name)], beside(axis, by))

    def jobs(kind, lo, n=1):
        whole = pl.ds(0, 4)
        for r in range(3):
            tiles = pl.ds(r * 12 + 3 * lo, 3 * n - ((r - lo - n + 1) % 3 == 2))
            axes = ORDERS[r]
            u, v, w = (pos[axis] for axis in axes)

            def at(*where, r=r, tiles=tiles):
                return region(r, tiles, *where)

            own = [at(u, v, w)]
            rest = [at(plus(u, j), v, w) for j in (1, 2, 3)]
            lines = [at(whole, plus(v, j), w) for j in (1, 2, 3)]
            if kind == "U":
                for k in (1, 2, 3):
                    yield (kind, r, lo, k), axes[0], k, (own,), at(plus(u, 4 - k), v, w)
            if kind == "V":
                for k in (1, 2, 3):
                    yield (kind, r, lo, k), axes[1], k, (own, rest), at(whole, plus(v, 4 - k), w)
            if kind in "AD":
                for k in (1, 2, 3) if kind == "D" else (1, 3):
                    yield (kind, r, lo, k), axes[2], k, (own, rest, lines), at(whole, whole, plus(w, 4 - k))
            if kind == "B":
                for k, half in ((1, pl.ds(0, 2)), (3, pl.ds(2, 2))):
                    parts = ([at(half, whole, plus(w, 4 - k))],)
                    yield (kind, r, lo, k), axes[2], k, parts, at(half, whole, plus(w, 2))

    def start(step, *what):
        for name, axis, k, parts, _ in jobs(*what):
            for ref in parts[step]:
                gather_copy(ref, name, axis, k).start()

    def arrive(*what):
        for name, axis, _, _, ref in jobs(*what):
            gather_copy(ref, name, axis, 1).wait_recv()

    def left(*what):
        for name, axis, _, _, ref in jobs(*what):
            gather_copy(ref, name, axis, 1).wait_send()

    def line(q):
        g, s = gain[pl.ds(core, 1)], shift[pl.ds(core, 1)]
        R = 256

        @pl.when(core == 0)
        def _():
            def step(i, _):
                rr = pl.ds(pl.multiple_of(i * R, R), R)
                src = pair[q, rr, :] if q < 2 else rowsbuf[q - 2, rr, :]
                lnorm[rr, :] = norm(src.astype(F32), g, s)
                return 0

            lax.fori_loop(0, N // R, step, 0)

        @pl.when(core == 1)
        def _():
            def step(i, _):
                rr = pl.ds(pl.multiple_of(i * R, R), R)
                v = cols[pl.ds(i * (R // 8), R // 8), q // 2 * 16 : q // 2 * 16 + 16, :].astype(F32)
                lnorm[rr, :] = norm(v[:, q % 2 * 8 : q % 2 * 8 + 8, :].reshape(R, 128), g, s)
                return 0

            lax.fori_loop(0, N // R, step, 0)

        def step(i, _):
            rr = pl.ds(pl.multiple_of(i * R, R), R)
            full = jnp.dot(lnorm[rr, :], wq[q], preferred_element_type=F32)
            qr[q, rr, :] = (full[:, :128] * DH**-0.5).astype(BF)
            k = full[:, 128:256].astype(BF)
            v = full[:, 256:384].astype(BF)
            for h in range(4):
                sl = slice(32 * ((q + h) % 4), 32 * ((q + h) % 4) + 32)
                kp[h, rr, sl] = k[:, sl]
                vp[h, rr, sl] = v[:, sl]
            gate[q, rr, :] = jax.nn.sigmoid(full[:, 384:] + gb[q, 0:1])
            return 0

        lax.fori_loop(0, N // R, step, 0)

        @pl.when(core == 0)
        def _():
            kt = lax.dot_general(wkt[q], lnorm[...], NT, preferred_element_type=F32).astype(BF)
            for h in range(4):
                s = (q + h) % 4
                kpt[h, 32 * s : 32 * s + 32, :] = kt[32 * s : 32 * s + 32, :]

    start(0, "U", 0)
    start(0, "U", 1, 3)
    start(0, "V", 0)
    start(0, "D", 0)
    picked_send()
    for what in (("V", 1), ("D", 1), ("V", 2, 2), ("A", 2), ("A", 3)):
        start(0, *what)
    arrive("U", 0)
    start(1, "V", 0)
    start(1, "D", 0)
    arrive("U", 1, 3)
    start(1, "V", 1)

    @pl.when(core == 0)
    def _():
        rows_copy.wait_recv()

    arrive("V", 0)
    start(2, "D", 0)
    start(1, "V", 2, 2)
    start(1, "D", 1)
    picked_end()
    line(0)
    arrive("V", 1)
    start(2, "D", 1)
    line(1)
    start(1, "A", 2)
    start(1, "A", 3)
    arrive("V", 2, 2)
    start(2, "A", 2)
    start(2, "A", 3)
    line(2)
    line(3)
    arrive("D", 0)

    lane = lax.broadcasted_iota(jnp.int32, (128, 128), 1)
    sub = lax.broadcasted_iota(jnp.int32, (128, 128), 0)
    slot = lane // 32

    def scores(c, h, jb, S, M):
        rows = pl.ds(pl.multiple_of(jb * 128, 128), 128)
        eye = (lane == sub).astype(F32).astype(BF)
        lhs = []
        for q in range(4):
            m = (slot == lax.rem(q + h, 4)).astype(F32).astype(BF)
            lhs.append(jnp.concatenate([qr[q, rows, :] * m, eye], 1))
        lhs = jnp.concatenate(lhs, 0)
        top = None
        for n in range(4):
            if c == 0:
                b = jnp.concatenate(
                    [
                        G[jb // 2, pl.ds(lax.rem(jb, 2) * 2, 2), :, tile_at(h, lt)].reshape(128, 128)
                        for lt in (2 * n, 2 * n + 1)
                    ],
                    1,
                )
                rhs = jnp.concatenate([kpt[h, :, n * 256 : (n + 1) * 256], b], 0)
                s = jnp.dot(lhs, rhs, preferred_element_type=F32)
            else:
                b = G[n, :, :, tile_at(h, jb)].reshape(256, 128)
                rhs = jnp.concatenate([kp[h, n * 256 : (n + 1) * 256, :], b], 1)
                s = lax.dot_general(lhs, rhs, NT, preferred_element_type=F32)
            S[:, n * 256 : (n + 1) * 256] = s
            t = jnp.maximum(s[:, :128], s[:, 128:])
            top = t if top is None else jnp.maximum(top, t)
        M[...] = jnp.broadcast_to(jnp.max(top, -1, keepdims=True), (512, 128))

    def mix(h, jb, S, M):
        rows = pl.ds(pl.multiple_of(jb * 128, 128), 128)
        p = jnp.exp(S[...] - jnp.concatenate([M[...]] * 8, 1)).astype(BF)
        o = jnp.dot(p, vp[h], preferred_element_type=F32)
        for q in range(4):
            oq = o[q * 128 : (q + 1) * 128]
            val = oq[:, :128] / oq[:, 128:] * gate[q, rows, :]
            acc[q, rows, :] = jnp.where(slot == lax.rem(q + h, 4), val, acc[q, rows, :])

    def finish(c, u0):
        first = pl.multiple_of(lax.rem(u0, 8) * 128, 256)
        rows = pl.ds(first, 256)
        for q in range(4):
            o = jnp.dot(acc[q, rows, :].astype(BF), wo[q], preferred_element_type=F32)
            ost[q, rows, :] = (o + out_bias[c : c + 1]).astype(BF)
        out = (out0, out1)[c].at[:, rows]
        remote(ost.at[pl.ds(2 - 2 * c, 2), rows], out, ms_s.at[2 + c], ms_r.at[2 + c], partner).start()
        pltpu.make_async_copy(ost.at[pl.ds(2 * c, 2), rows], out, ms_s.at[4]).start()

    for c in range(2):
        pl.when(core == c)(lambda c=c: scores(c, 0, 0, sA, mA))

    def pair_of_units(i, _):
        @pl.when(i == 3)
        def _():
            arrive("D", 1)

        @pl.when(i == 4)
        def _():
            arrive("A", 2)
            start(0, "B", 2)

        @pl.when(i == 6)
        def _():
            arrive("A", 3)
            start(0, "B", 3)

        @pl.when(i == 7)
        def _():
            arrive("B", 2)

        @pl.when(i == 11)
        def _():
            arrive("B", 3)

        u0 = 2 * i
        u1 = u0 + 1
        u2 = lax.rem(u0 + 2, 32)
        for c in range(2):

            @pl.when(core == c)
            def _(c=c):
                scores(c, u1 // 8, lax.rem(u1, 8), sB, mB)
                mix(u0 // 8, lax.rem(u0, 8), sA, mA)
                scores(c, u2 // 8, lax.rem(u2, 8), sA, mA)
                mix(u1 // 8, lax.rem(u1, 8), sB, mB)
                pl.when(i >= 12)(lambda: finish(c, u0))

        return 0

    lax.fori_loop(0, 16, pair_of_units, 0)

    for c, out in ((0, out0), (1, out1)):

        @pl.when(core == c)
        def _(c=c, out=out):
            pltpu.make_async_copy(ost.at[pl.ds(2 * c, 2)], out, ms_s.at[4]).wait()
            remote(ost.at[pl.ds(2 - 2 * c, 2)], out, ms_s.at[2 + c], ms_r.at[2 + c], partner).wait_send()

    for c, out in ((1, out0), (0, out1)):

        @pl.when(core == c)
        def _(c=c, out=out):
            remote(ost.at[pl.ds(0, 2)], out, ms_s.at[3 - c], ms_r.at[3 - c], partner).wait_recv()

    half_copy.wait_send()

    @pl.when(core == 0)
    def _():
        remote(pk, pk, aa_s, aa_r, partner).wait_send()

    @pl.when(core == 1)
    def _():
        most = pk.at[pl.ds(0, 63)]
        remote(most, most, aa_s, aa_r, partner).wait_send()
        rows_copy.wait_send()

    for what in (
        ("U", 0), ("U", 1, 3), ("V", 0), ("V", 1), ("V", 2, 2), ("D", 0), ("D", 1), ("A", 2), ("A", 3), ("B", 2), ("B", 3)
    ):
        left(*what)


def hand_over(a, b, out0, out1, sems):
    copies = [pltpu.make_async_copy(a, out0, sems.at[0]), pltpu.make_async_copy(b, out1, sems.at[1])]
    for copy in copies:
        copy.start()
    for copy in copies:
        copy.wait()


def local(pair, residue_mask, ln_gain, ln_shift, w_proj, w_bias, gate_bias, w_out, out_bias):
    vmem = pl.BlockSpec(memory_space=pltpu.VMEM)
    out = jax.ShapeDtypeStruct((2, N, C), BF)
    V = pltpu.VMEM
    dma = pltpu.SemaphoreType.DMA
    anywhere = pl.BlockSpec(memory_space=pl.ANY)
    raw = pl.pallas_call(
        body,
        out_shape=(out, out),
        in_specs=[anywhere] + [vmem] * 8,
        out_specs=(anywhere,) * 2,
        scratch_shapes=[
            V((4, 4, 4, 36, 16, 128), BF), V((RD, N, C), BF), V((N, C), F32), V((2048, C), F32), V((64, 32, C), BF),
            V((128, 32, C), BF),
            V((2, N, C), BF), V((64, N), F32), V((32, N), F32),
            V((4, 128, 512), BF), V((4, 128, 128), BF), V((4, 8, 128), F32), V((4, 128, 128), BF), V((N, C), BF),
            V((4, N, C), BF), V((4, N, C), BF), V((4, C, N), BF), V((4, N, 256), BF), V((4, N, C), F32), V((4, N, C), F32),
            V((512, N), F32), V((512, N), F32), V((512, 128), F32), V((512, 128), F32), V((4, N, C), BF),
            dma((120,)), dma((120,)), dma, dma, dma((5,)), dma((4,)), dma((8,)),
        ],
        compiler_params=pltpu.CompilerParams(
            collective_id=0, has_side_effects=True, vmem_limit_bytes=56 * 2**20
        ),
        cost_estimate=pl.CostEstimate(flops=20 * 10**9, bytes_accessed=4 * 2**20, transcendentals=17 * 10**6),
    )(pair, residue_mask.reshape(1, N), ln_gain, ln_shift, w_proj, jnp.transpose(w_bias, (0, 2, 1)), gate_bias, w_out, out_bias)
    return pl.pallas_call(
        hand_over, out_shape=(out, out), in_specs=[vmem] * 2, out_specs=(anywhere,) * 2, scratch_shapes=[dma((2,))]
    )(*raw)


def solution(mesh):
    return jax.shard_map(
        local,
        mesh=mesh,
        in_specs=(P(("row", "col"), None, None), P(), P(), P(), P(), P(), P(), P(), P()),
        out_specs=(P(("row", "col"), None, None), P(("row", "col"), None, None)),
        check_vma=False,
    )
```

```python
import jax
import jax.numpy as jnp
from jax import lax
from jax.experimental import pallas as pl
from jax.experimental.pallas import tpu as pltpu
from jax.sharding import PartitionSpec as P

N, C, HEADS, DH, RD = 1024, 128, 4, 32, 8
BF, F32 = jnp.bfloat16, jnp.float32
MESH = pl.DeviceIdType.MESH
NT = (((1,), (1,)), ((), ()))
NEG = -1e30
EPS = 1e-05
ORDERS = ((2, 1, 0), (0, 2, 1), (1, 0, 2))
PICKED = (0, 1, 8, 9)


def tile_at(h, lt):
    if isinstance(h, int) and isinstance(lt, int):
        return (lt // 3 + h) % 3 * 12 + h * 3 + lt % 3
    return lax.rem(lt // 3 + h, 3) * 12 + h * 3 + lax.rem(lt, 3)


def device_of(z, x, y, core):
    return (z * 2 + x // 2, lax.rem(x, 2) * 8 + y * 2 + core)


def stats_norm(x):
    ones = jnp.ones((2 * C, C), BF)
    d = x.astype(F32) - jnp.dot(x, ones[:C], preferred_element_type=F32) * (1 / C)
    square = d * d
    high = square.astype(BF)
    low = (square - high.astype(F32)).astype(BF)
    spread = jnp.dot(jnp.concatenate([high, low], 1), ones, preferred_element_type=F32) * (1 / C)
    return d * lax.rsqrt(spread + EPS)


def norm(x, gain, shift):
    return (stats_norm(x) * gain + shift).astype(BF)


def body(
    pair_hbm, mask, gain, shift, w_proj, w_bias, gate_bias, w_out, out_bias,
    out0, out1,
    G, pair, xf, pkf, pk, cols, rowsbuf, bacc, xb,
    wq, wo, gb, qr, kp, kpt, vp, gate, acc, sA, sB, mA, mB, ost,
    ag_s, ag_r, aa_s, aa_r, ms_s, ms_r, ld_s,
):
    row, col = lax.axis_index("row"), lax.axis_index("col")
    me = row * 16 + col
    z, x = row // 2, lax.rem(row, 2) * 2 + col // 8
    y, core = lax.rem(col // 2, 4), lax.rem(col, 2)
    pos = (z, x, y)
    partner = (row, col + 1 - 2 * core)
    barrier = pltpu.get_barrier_semaphore()

    def signal(dev):
        pl.semaphore_signal(barrier, inc=1, device_id=dev, device_id_type=MESH)

    def beside(axis, by):
        p = list(pos)
        p[axis] = lax.rem(p[axis] + by, 4)
        return device_of(*p, core)

    def load(a):
        return pltpu.make_async_copy(pair_hbm.at[a], pair.at[a], ld_s.at[a])

    for a in range(RD):
        load(a).start()

    @pl.when(core == 0)
    def _():
        signal(partner)
        for axis in range(3):
            for by in (1, 2, 3):
                signal(beside(axis, by))

    @pl.when(core == 1)
    def _():
        def one(i, _):
            d = lax.rem(me + i, 128)
            signal((d // 16, lax.rem(d, 16)))
            return 0

        lax.fori_loop(1, 128, one, 0)

    def pick(a):
        load(a).wait()
        xf[...] = pair[a].astype(F32)
        for q in range(4):
            pkf[pl.ds(q * 8 + a, 64, stride=32), :] = xf[pl.ds(PICKED[q], 64, stride=16), :]

    for a in range(RD):
        pick(a)

    def pack(i, _):
        pk[pl.ds(i * 8, 8)] = pkf[pl.ds(pl.multiple_of(i * 256, 256), 256), :].reshape(8, 32, 128).astype(BF)
        return 0

    lax.fori_loop(0, 8, pack, 0)

    def remote(src, dst, send, recv, dev):
        return pltpu.make_async_remote_copy(src, dst, send, recv, device_id=dev, device_id_type=MESH)

    def plus(v, k):
        return lax.rem(v + k, 4)

    def picked_send():
        chip = me // 2

        def one(i, _):
            c = lax.rem(chip + i, 64)
            remote(pk.at[c], cols.at[me], aa_s, aa_r, (c // 8, lax.rem(c, 8) * 2 + 1)).start()
            return 0

        lax.fori_loop(1, 64, one, 0)

        @pl.when(core == 0)
        def _():
            remote(pk.at[chip], cols.at[me], aa_s, aa_r, partner).start()

        @pl.when(core == 1)
        def _():
            cols[me] = pk[chip]

    def picked_end():
        @pl.when(core == 1)
        def _():
            every = cols.at[pl.ds(0, 127)]
            remote(every, every, aa_s, aa_r, partner).wait_recv()

    rows_copy = remote(pair.at[pl.ds(0, 2)], rowsbuf, ms_s.at[0], ms_r.at[0], partner)

    wcat = []
    for p in range(2):
        wcat.append(w_bias[p].astype(F32))
    zero8 = jnp.zeros((8, 128), F32)
    wrep = jnp.concatenate(
        [
            jnp.concatenate(
                [jnp.broadcast_to(wcat[p][h : h + 1], (8, 128)) if s == p else zero8 for s in range(2)], 1
            )
            for p in range(2)
            for h in range(4)
        ],
        0,
    )
    r8 = lax.rem(lax.broadcasted_iota(jnp.int32, (64, 256), 0), 8)

    def bias_row(a, _):
        lhs = jnp.where(r8 == a, wrep, 0.0).astype(BF)
        xn = stats_norm(pair[a])
        both = jnp.concatenate([(xn * gain[p : p + 1] + shift[p : p + 1]).astype(BF) for p in range(2)], 1)
        bacc[...] += lax.dot_general(lhs, both, NT, preferred_element_type=F32)
        return 0

    bacc[...] = jnp.zeros((64, N), F32)
    lax.fori_loop(0, RD, bias_row, 0)
    live = jnp.broadcast_to(mask[...], (8, N))
    lane8 = lax.broadcasted_iota(jnp.int32, (8, N), 1)
    sub8 = lax.broadcasted_iota(jnp.int32, (8, N), 0)
    own = jnp.sum(jnp.where(lane8 == me * 8 + sub8, live, 0), -1, keepdims=True)
    own = jnp.broadcast_to(own, (8, N))
    for ph in range(8):
        keep = (live if ph < 4 else own) > 0
        bacc[ph * 8 : ph * 8 + 8, :] = jnp.where(keep, bacc[ph * 8 : ph * 8 + 8, :], NEG)
    half_copy = pltpu.make_async_remote_copy(
        bacc.at[pl.ds(pl.multiple_of((1 - core) * 32, 32), 32)],
        xb, ms_s.at[1], ms_r.at[1], device_id=partner, device_id_type=MESH,
    )
    pl.semaphore_wait(barrier, 73 - 9 * core)
    half_copy.start()

    @pl.when(core == 1)
    def _():
        rows_copy.start()

    def prep_weights():
        for q in range(4):
            for blk in range(4):
                w = w_proj[core, :, blk * 128 : (blk + 1) * 128].astype(F32)
                if q:
                    w = pltpu.roll(w, 32 * q, 1)
                wq[q, :, blk * 128 : (blk + 1) * 128] = w.astype(BF)
            o = w_out[core].astype(F32)
            g = jnp.broadcast_to(gate_bias[pl.ds(core, 1)], (8, 128))
            if q:
                o = pltpu.roll(o, 32 * q, 0)
                g = pltpu.roll(g, 32 * q, 1)
            wo[q] = o.astype(BF)
            gb[q] = g
        vp[:, :, 128:] = jnp.ones((4, N, 128), BF)
        acc[...] = jnp.zeros_like(acc)

    prep_weights()

    half_copy.wait_recv()
    mine = pl.multiple_of(core * 32, 32)
    for h in range(4):
        ours = bacc[pl.ds(pl.multiple_of(mine + h * 8, 8), 8), :]
        theirs = xb[h * 8 : h * 8 + 8, :]
        low = jnp.where(core == 0, ours, theirs)
        high = jnp.where(core == 0, theirs, ours)
        block = jnp.concatenate([low, high], 0).astype(BF)
        for lt in range(8):
            G[z, x, y, tile_at(h, lt)] = block[:, lt * 128 : (lt + 1) * 128]
    for r in range(3):
        for h in range(4):
            if (r - h) % 3 == 2:
                G[z, x, y, r * 12 + h * 3 + 2] = jnp.zeros((16, 128), BF)

    names = {}

    def sem(*name):
        return names.setdefault(name, len(names))

    def region(r, tiles, u, v, w):
        index = [0, 0, 0]
        for axis, at in zip(ORDERS[r], (u, v, w)):
            index[axis] = at
        return G.at[index[0], index[1], index[2], tiles]

    def gather_copy(ref, name, axis, by):
        return remote(ref, ref, ag_s.at[sem(*name)], ag_r.at[sem(*name)], beside(axis, by))

    def jobs(kind, lo, n=1):
        whole = pl.ds(0, 4)
        for r in range(3):
            tiles = pl.ds(r * 12 + 3 * lo, 3 * n - ((r - lo - n + 1) % 3 == 2))
            axes = ORDERS[r]
            u, v, w = (pos[axis] for axis in axes)

            def at(*where, r=r, tiles=tiles):
                return region(r, tiles, *where)

            own = [at(u, v, w)]
            rest = [at(plus(u, j), v, w) for j in (1, 2, 3)]
            lines = [at(whole, plus(v, j), w) for j in (1, 2, 3)]
            if kind == "U":
                for k in (1, 2, 3):
                    yield (kind, r, lo, k), axes[0], k, (own,), at(plus(u, 4 - k), v, w)
            if kind == "V":
                for k in (1, 2, 3):
                    yield (kind, r, lo, k), axes[1], k, (own, rest), at(whole, plus(v, 4 - k), w)
            if kind in "AD":
                for k in (1, 2, 3) if kind == "D" else (1, 3):
                    yield (kind, r, lo, k), axes[2], k, (own, rest, lines), at(whole, whole, plus(w, 4 - k))
            if kind == "B":
                for k, half in ((1, pl.ds(0, 2)), (3, pl.ds(2, 2))):
                    parts = ([at(half, whole, plus(w, 4 - k))],)
                    yield (kind, r, lo, k), axes[2], k, parts, at(half, whole, plus(w, 2))

    def start(step, *what):
        for name, axis, k, parts, _ in jobs(*what):
            for ref in parts[step]:
                gather_copy(ref, name, axis, k).start()

    def arrive(*what):
        for name, axis, _, _, ref in jobs(*what):
            gather_copy(ref, name, axis, 1).wait_recv()

    def start_all(*what):
        for name, axis, k, parts, _ in jobs(*what):
            for step in parts:
                for ref in step:
                    gather_copy(ref, name, axis, k).start()

    def left(*what):
        for name, axis, _, _, ref in jobs(*what):
            gather_copy(ref, name, axis, 1).wait_send()

    def line(q):
        g, s = gain[pl.ds(core, 1)], shift[pl.ds(core, 1)]

        def project(rows):
            full = jnp.dot(norm(rows, g, s), wq[q], preferred_element_type=F32)
            qr[q] = (full[:, :128] * DH**-0.5).astype(BF)
            v = full[:, 256:384].astype(BF)
            for h in range(4):
                sl = slice(32 * ((q + h) % 4), 32 * ((q + h) % 4) + 32)
                vp[h, :, sl] = v[:, sl]
            gate[q] = jax.nn.sigmoid(full[:, 384:] + gb[q, 0:1])
            return full[:, 128:256].astype(BF)

        @pl.when(core == 0)
        def _():
            kt = jnp.transpose(project(pair[q] if q < 2 else rowsbuf[q - 2]))
            for h in range(4):
                sl = slice(32 * ((q + h) % 4), 32 * ((q + h) % 4) + 32)
                kpt[h, sl, :] = kt[sl]

        @pl.when(core == 1)
        def _():
            rows = cols[:, q // 2 * 16 : q // 2 * 16 + 16, :].astype(F32)
            k = project(rows[:, q % 2 * 8 : q % 2 * 8 + 8, :].reshape(N, C).astype(BF))
            for h in range(4):
                sl = slice(32 * ((q + h) % 4), 32 * ((q + h) % 4) + 32)
                kp[h, :, sl] = k[:, sl]

    def rows_ready():
        @pl.when(core == 0)
        def _():
            rows_copy.wait_recv()

    start(0, "U", 0)
    start(0, "U", 1, 3)
    picked_send()
    arrive("U", 0)
    start_all("V", 0)
    arrive("U", 1, 3)
    start_all("V", 1, 3)
    rows_ready()
    arrive("V", 0)
    start_all("A", 0)
    arrive("V", 1, 3)
    start_all("A", 1)
    picked_end()
    line(0)
    line(1)
    line(2)
    line(3)
    arrive("A", 0)
    start(0, "B", 0)
    start_all("A", 2)
    arrive("A", 1)
    start(0, "B", 1)
    arrive("B", 0)

    lane = lax.broadcasted_iota(jnp.int32, (128, 128), 1)
    sub = lax.broadcasted_iota(jnp.int32, (128, 128), 0)
    slot = lane // 32
    slot2 = lax.broadcasted_iota(jnp.int32, (256, 128), 1) // 32

    def scores(c, p, S, M):
        for part in range(2):
            half = pl.ds(512 * part, 512)
            scores_of(c, p // 4, lax.rem(p, 4) * 2 + part, S.at[half], M.at[half])

    def scores_of(c, h, jb, S, M):
        rows = pl.ds(pl.multiple_of(jb * 128, 128), 128)
        eye = (lane == sub).astype(F32).astype(BF)
        lhs = []
        for q in range(4):
            m = (slot == lax.rem(q + h, 4)).astype(F32).astype(BF)
            lhs.append(jnp.concatenate([qr[q, rows, :] * m, eye], 1))
        lhs = jnp.concatenate(lhs, 0)
        top = None
        for n in range(4):
            if c == 0:
                b = jnp.concatenate(
                    [
                        G[jb // 2, pl.ds(lax.rem(jb, 2) * 2, 2), :, tile_at(h, lt)].reshape(128, 128)
                        for lt in (2 * n, 2 * n + 1)
                    ],
                    1,
                )
                rhs = jnp.concatenate([kpt[h, :, n * 256 : (n + 1) * 256], b], 0)
                s = jnp.dot(lhs, rhs, preferred_element_type=F32)
            else:
                b = G[n, :, :, tile_at(h, jb)].reshape(256, 128)
                rhs = jnp.concatenate([kp[h, n * 256 : (n + 1) * 256, :], b], 1)
                s = lax.dot_general(lhs, rhs, NT, preferred_element_type=F32)
            S[:, n * 256 : (n + 1) * 256] = s
            t = jnp.maximum(s[:, :128], s[:, 128:])
            top = t if top is None else jnp.maximum(top, t)
        M[...] = jnp.broadcast_to(jnp.max(top, -1, keepdims=True), (512, 128))

    def mix(p, S, M):
        h, rows = p // 4, pl.ds(pl.multiple_of(lax.rem(p, 4) * 256, 256), 256)
        weights = jnp.exp(S[...] - jnp.concatenate([M[...]] * 8, 1)).astype(BF)
        o = jnp.dot(weights, vp[h], preferred_element_type=F32)
        for q in range(4):
            oq = jnp.concatenate([o[q * 128 : (q + 1) * 128], o[512 + q * 128 : 640 + q * 128]], 0)
            val = oq[:, :128] / oq[:, 128:] * gate[q, rows, :]
            acc[q, rows, :] = jnp.where(slot2 == lax.rem(q + h, 4), val, acc[q, rows, :])

    def finish(c, p):
        rows = pl.ds(pl.multiple_of(lax.rem(p, 4) * 256, 256), 256)
        for q in range(4):
            o = jnp.dot(acc[q, rows, :].astype(BF), wo[q], preferred_element_type=F32)
            ost[q, rows, :] = (o + out_bias[c : c + 1]).astype(BF)
        out = (out0, out1)[c].at[:, rows]
        remote(ost.at[pl.ds(2 - 2 * c, 2), rows], out, ms_s.at[2 + c], ms_r.at[2 + c], partner).start()
        pltpu.make_async_copy(ost.at[pl.ds(2 * c, 2), rows], out, ms_s.at[4]).start()

    for c in range(2):
        pl.when(core == c)(lambda c=c: scores(c, 0, sA, mA))

    def event0():
        start_all("A", 3)

    def event2():
        arrive("A", 2)
        start(0, "B", 2)

    def event3():
        arrive("B", 1)

    def event6():
        arrive("A", 3)
        start(0, "B", 3)

    def event7():
        arrive("B", 2)

    def event11():
        arrive("B", 3)

    events = {0: event0, 2: event2, 3: event3, 6: event6, 7: event7, 11: event11}

    def pairs(i, _):
        for odd in range(2):
            p = 2 * i + odd
            for when, event in events.items():
                if when % 2 == odd:
                    pl.when(i == when // 2)(event)
            now, later = ((sA, mA), (sB, mB))[:: 1 - 2 * odd]
            for c in range(2):

                @pl.when(core == c)
                def _(c=c, p=p, now=now, later=later):
                    scores(c, lax.rem(p + 1, 16), *later)
                    mix(p, *now)
                    pl.when(i >= 6)(lambda: finish(c, p))

        return 0

    lax.fori_loop(0, 8, pairs, 0)

    for c, out in ((0, out0), (1, out1)):

        @pl.when(core == c)
        def _(c=c, out=out):
            pltpu.make_async_copy(ost.at[pl.ds(2 * c, 2)], out, ms_s.at[4]).wait()
            remote(ost.at[pl.ds(2 - 2 * c, 2)], out, ms_s.at[2 + c], ms_r.at[2 + c], partner).wait_send()

    for c, out in ((1, out0), (0, out1)):

        @pl.when(core == c)
        def _(c=c, out=out):
            remote(ost.at[pl.ds(0, 2)], out, ms_s.at[3 - c], ms_r.at[3 - c], partner).wait_recv()

    half_copy.wait_send()

    @pl.when(core == 0)
    def _():
        remote(pk, pk, aa_s, aa_r, partner).wait_send()

    @pl.when(core == 1)
    def _():
        most = pk.at[pl.ds(0, 63)]
        remote(most, most, aa_s, aa_r, partner).wait_send()
        rows_copy.wait_send()

    for what in (
        ("U", 0), ("U", 1, 3), ("V", 0), ("V", 1, 3), ("A", 0), ("A", 1), ("B", 0), ("A", 2), ("B", 1), ("A", 3), ("B", 2), ("B", 3)
    ):
        left(*what)


def hand_over(a, b, out0, out1, sems):
    copies = [pltpu.make_async_copy(a, out0, sems.at[0]), pltpu.make_async_copy(b, out1, sems.at[1])]
    for copy in copies:
        copy.start()
    for copy in copies:
        copy.wait()


def local(pair, residue_mask, ln_gain, ln_shift, w_proj, w_bias, gate_bias, w_out, out_bias):
    vmem = pl.BlockSpec(memory_space=pltpu.VMEM)
    out = jax.ShapeDtypeStruct((2, N, C), BF)
    V = pltpu.VMEM
    dma = pltpu.SemaphoreType.DMA
    anywhere = pl.BlockSpec(memory_space=pl.ANY)
    raw = pl.pallas_call(
        body,
        out_shape=(out, out),
        in_specs=[anywhere] + [vmem] * 8,
        out_specs=(anywhere,) * 2,
        scratch_shapes=[
            V((4, 4, 4, 36, 16, 128), BF), V((RD, N, C), BF), V((N, C), F32), V((2048, C), F32), V((64, 32, C), BF),
            V((128, 32, C), BF),
            V((2, N, C), BF), V((64, N), F32), V((32, N), F32),
            V((4, 128, 512), BF), V((4, 128, 128), BF), V((4, 8, 128), F32),
            V((4, N, C), BF), V((4, N, C), BF), V((4, C, N), BF), V((4, N, 256), BF), V((4, N, C), F32), V((4, N, C), F32),
            V((1024, N), F32), V((1024, N), F32), V((1024, 128), F32), V((1024, 128), F32), V((4, N, C), BF),
            dma((120,)), dma((120,)), dma, dma, dma((5,)), dma((4,)), dma((8,)),
        ],
        compiler_params=pltpu.CompilerParams(
            collective_id=0, has_side_effects=True, vmem_limit_bytes=56 * 2**20
        ),
        cost_estimate=pl.CostEstimate(flops=20 * 10**9, bytes_accessed=4 * 2**20, transcendentals=17 * 10**6),
    )(pair, residue_mask.reshape(1, N), ln_gain, ln_shift, w_proj, jnp.transpose(w_bias, (0, 2, 1)), gate_bias, w_out, out_bias)
    return pl.pallas_call(
        hand_over, out_shape=(out, out), in_specs=[vmem] * 2, out_specs=(anywhere,) * 2, scratch_shapes=[dma((2,))]
    )(*raw)


def solution(mesh):
    return jax.shard_map(
        local,
        mesh=mesh,
        in_specs=(P(("row", "col"), None, None), P(), P(), P(), P(), P(), P(), P(), P()),
        out_specs=(P(("row", "col"), None, None), P(("row", "col"), None, None)),
        check_vma=False,
    )
```

```python
import jax
import jax.numpy as jnp
from jax import lax
from jax.experimental import pallas as pl
from jax.experimental.pallas import tpu as pltpu
from jax.sharding import PartitionSpec as P

N, C, HEADS, DH, RD = 1024, 128, 4, 32, 8
BF, F32 = jnp.bfloat16, jnp.float32
MESH = pl.DeviceIdType.MESH
NT = (((1,), (1,)), ((), ()))
NEG = -1e30
EPS = 1e-05
ORDERS = ((2, 1, 0), (0, 2, 1), (1, 0, 2))
PICKED = (0, 1, 8, 9)


def tile_at(h, lt):
    if isinstance(h, int) and isinstance(lt, int):
        return (lt // 3 + h) % 3 * 12 + h * 3 + lt % 3
    return lax.rem(lt // 3 + h, 3) * 12 + h * 3 + lax.rem(lt, 3)


def device_of(z, x, y, core):
    return (z * 2 + x // 2, lax.rem(x, 2) * 8 + y * 2 + core)


def stats_norm(x):
    ones = jnp.ones((2 * C, C), BF)
    d = x.astype(F32) - jnp.dot(x, ones[:C], preferred_element_type=F32) * (1 / C)
    square = d * d
    high = square.astype(BF)
    low = (square - high.astype(F32)).astype(BF)
    spread = jnp.dot(jnp.concatenate([high, low], 1), ones, preferred_element_type=F32) * (1 / C)
    return d * lax.rsqrt(spread + EPS)


def norm(x, gain, shift):
    return (stats_norm(x) * gain + shift).astype(BF)


def body(
    pair_hbm, mask, gain, shift, w_proj, w_bias, gate_bias, w_out, out_bias,
    out0, out1,
    G, pair, xf, pkf, pk, cols, rowsbuf, bacc, xb,
    wq, wo, gb, qr, kp, kpt, vp, gate, acc, sA, sB, mA, mB, ost,
    ag_s, ag_r, aa_s, aa_r, ms_s, ms_r, ld_s,
):
    row, col = lax.axis_index("row"), lax.axis_index("col")
    me = row * 16 + col
    z, x = row // 2, lax.rem(row, 2) * 2 + col // 8
    y, core = lax.rem(col // 2, 4), lax.rem(col, 2)
    pos = (z, x, y)
    partner = (row, col + 1 - 2 * core)
    barrier = pltpu.get_barrier_semaphore()

    def signal(dev):
        pl.semaphore_signal(barrier, inc=1, device_id=dev, device_id_type=MESH)

    def beside(axis, by):
        p = list(pos)
        p[axis] = lax.rem(p[axis] + by, 4)
        return device_of(*p, core)

    def load(a):
        return pltpu.make_async_copy(pair_hbm.at[a], pair.at[a], ld_s.at[a])

    for a in range(RD):
        load(a).start()

    @pl.when(core == 0)
    def _():
        signal(partner)
        for axis in range(3):
            for by in (1, 2, 3):
                signal(beside(axis, by))

    @pl.when(core == 1)
    def _():
        def one(i, _):
            d = lax.rem(me + i, 128)
            signal((d // 16, lax.rem(d, 16)))
            return 0

        lax.fori_loop(1, 128, one, 0)

    def pick(a):
        load(a).wait()
        xf[...] = pair[a].astype(F32)
        for q in range(4):
            pkf[pl.ds(q * 8 + a, 64, stride=32), :] = xf[pl.ds(PICKED[q], 64, stride=16), :]

    for a in range(RD):
        pick(a)

    def pack(i, _):
        pk[pl.ds(i * 8, 8)] = pkf[pl.ds(pl.multiple_of(i * 256, 256), 256), :].reshape(8, 32, 128).astype(BF)
        return 0

    lax.fori_loop(0, 8, pack, 0)

    def remote(src, dst, send, recv, dev):
        return pltpu.make_async_remote_copy(src, dst, send, recv, device_id=dev, device_id_type=MESH)

    def plus(v, k):
        return lax.rem(v + k, 4)

    def picked_send():
        chip = me // 2

        def one(i, _):
            c = lax.rem(chip + i, 64)
            remote(pk.at[c], cols.at[me], aa_s, aa_r, (c // 8, lax.rem(c, 8) * 2 + 1)).start()
            return 0

        lax.fori_loop(1, 64, one, 0)

        @pl.when(core == 0)
        def _():
            remote(pk.at[chip], cols.at[me], aa_s, aa_r, partner).start()

        @pl.when(core == 1)
        def _():
            cols[me] = pk[chip]

    def picked_end():
        @pl.when(core == 1)
        def _():
            every = cols.at[pl.ds(0, 127)]
            remote(every, every, aa_s, aa_r, partner).wait_recv()

    rows_copy = remote(pair.at[pl.ds(0, 2)], rowsbuf, ms_s.at[0], ms_r.at[0], partner)

    wcat = []
    for p in range(2):
        wcat.append(w_bias[p].astype(F32))
    zero8 = jnp.zeros((8, 128), F32)
    wrep = jnp.concatenate(
        [
            jnp.concatenate(
                [jnp.broadcast_to(wcat[p][h : h + 1], (8, 128)) if s == p else zero8 for s in range(2)], 1
            )
            for p in range(2)
            for h in range(4)
        ],
        0,
    )
    r8 = lax.rem(lax.broadcasted_iota(jnp.int32, (64, 256), 0), 8)

    def bias_row(a, _):
        lhs = jnp.where(r8 == a, wrep, 0.0).astype(BF)
        xn = stats_norm(pair[a])
        both = jnp.concatenate([(xn * gain[p : p + 1] + shift[p : p + 1]).astype(BF) for p in range(2)], 1)
        bacc[...] += lax.dot_general(lhs, both, NT, preferred_element_type=F32)
        return 0

    bacc[...] = jnp.zeros((64, N), F32)
    lax.fori_loop(0, RD, bias_row, 0)
    live = jnp.broadcast_to(mask[...], (8, N))
    lane8 = lax.broadcasted_iota(jnp.int32, (8, N), 1)
    sub8 = lax.broadcasted_iota(jnp.int32, (8, N), 0)
    own = jnp.sum(jnp.where(lane8 == me * 8 + sub8, live, 0), -1, keepdims=True)
    own = jnp.broadcast_to(own, (8, N))
    for ph in range(8):
        keep = (live if ph < 4 else own) > 0
        bacc[ph * 8 : ph * 8 + 8, :] = jnp.where(keep, bacc[ph * 8 : ph * 8 + 8, :], NEG)
    half_copy = pltpu.make_async_remote_copy(
        bacc.at[pl.ds(pl.multiple_of((1 - core) * 32, 32), 32)],
        xb, ms_s.at[1], ms_r.at[1], device_id=partner, device_id_type=MESH,
    )
    def prep_weights():
        for q in range(4):
            for blk in range(4):
                w = w_proj[core, :, blk * 128 : (blk + 1) * 128].astype(F32)
                if q:
                    w = pltpu.roll(w, 32 * q, 1)
                wq[q, :, blk * 128 : (blk + 1) * 128] = w.astype(BF)
            o = w_out[core].astype(F32)
            g = jnp.broadcast_to(gate_bias[pl.ds(core, 1)], (8, 128))
            if q:
                o = pltpu.roll(o, 32 * q, 0)
                g = pltpu.roll(g, 32 * q, 1)
            wo[q] = o.astype(BF)
            gb[q] = g
        vp[:, :, 128:] = jnp.ones((4, N, 128), BF)
        acc[...] = jnp.zeros_like(acc)

    prep_weights()
    pl.semaphore_wait(barrier, 73 - 9 * core)
    half_copy.start()

    @pl.when(core == 1)
    def _():
        rows_copy.start()

    half_copy.wait_recv()
    mine = pl.multiple_of(core * 32, 32)
    for h in range(4):
        ours = bacc[pl.ds(pl.multiple_of(mine + h * 8, 8), 8), :]
        theirs = xb[h * 8 : h * 8 + 8, :]
        low = jnp.where(core == 0, ours, theirs)
        high = jnp.where(core == 0, theirs, ours)
        block = jnp.concatenate([low, high], 0).astype(BF)
        for lt in range(8):
            G[z, x, y, tile_at(h, lt)] = block[:, lt * 128 : (lt + 1) * 128]
    for r in range(3):
        for h in range(4):
            if (r - h) % 3 == 2:
                G[z, x, y, r * 12 + h * 3 + 2] = jnp.zeros((16, 128), BF)

    names = {}

    def sem(*name):
        return names.setdefault(name, len(names))

    def region(r, tiles, u, v, w):
        index = [0, 0, 0]
        for axis, at in zip(ORDERS[r], (u, v, w)):
            index[axis] = at
        return G.at[index[0], index[1], index[2], tiles]

    def gather_copy(ref, name, axis, by):
        return remote(ref, ref, ag_s.at[sem(*name)], ag_r.at[sem(*name)], beside(axis, by))

    def jobs(kind, lo, n=1):
        whole = pl.ds(0, 4)
        for r in range(3):
            tiles = pl.ds(r * 12 + 3 * lo, 3 * n - ((r - lo - n + 1) % 3 == 2))
            axes = ORDERS[r]
            u, v, w = (pos[axis] for axis in axes)

            def at(*where, r=r, tiles=tiles):
                return region(r, tiles, *where)

            own = [at(u, v, w)]
            rest = [at(plus(u, j), v, w) for j in (1, 2, 3)]
            lines = [at(whole, plus(v, j), w) for j in (1, 2, 3)]
            if kind == "U":
                for k in (1, 2, 3):
                    yield (kind, r, lo, k), axes[0], k, (own,), at(plus(u, 4 - k), v, w)
            if kind == "V":
                for k in (1, 2, 3):
                    yield (kind, r, lo, k), axes[1], k, (own, rest), at(whole, plus(v, 4 - k), w)
            if kind in "AD":
                for k in (1, 2, 3) if kind == "D" else (1, 3):
                    yield (kind, r, lo, k), axes[2], k, (own, rest, lines), at(whole, whole, plus(w, 4 - k))
            if kind == "B":
                for k, half in ((1, pl.ds(0, 2)), (3, pl.ds(2, 2))):
                    parts = ([at(half, whole, plus(w, 4 - k))],)
                    yield (kind, r, lo, k), axes[2], k, parts, at(half, whole, plus(w, 2))

    def start(step, *what):
        for name, axis, k, parts, _ in jobs(*what):
            for ref in parts[step]:
                gather_copy(ref, name, axis, k).start()

    def arrive(*what):
        for name, axis, _, _, ref in jobs(*what):
            gather_copy(ref, name, axis, 1).wait_recv()

    def start_all(*what):
        for name, axis, k, parts, _ in jobs(*what):
            for step in parts:
                for ref in step:
                    gather_copy(ref, name, axis, k).start()

    def left(*what):
        for name, axis, _, _, ref in jobs(*what):
            gather_copy(ref, name, axis, 1).wait_send()

    def line(q):
        g, s = gain[pl.ds(core, 1)], shift[pl.ds(core, 1)]

        def project(rows):
            full = jnp.dot(norm(rows, g, s), wq[q], preferred_element_type=F32)
            qr[q] = (full[:, :128] * DH**-0.5).astype(BF)
            v = full[:, 256:384].astype(BF)
            for h in range(4):
                sl = slice(32 * ((q + h) % 4), 32 * ((q + h) % 4) + 32)
                vp[h, :, sl] = v[:, sl]
            gate[q] = jax.nn.sigmoid(full[:, 384:] + gb[q, 0:1])
            return full[:, 128:256].astype(BF)

        @pl.when(core == 0)
        def _():
            kt = jnp.transpose(project(pair[q] if q < 2 else rowsbuf[q - 2]))
            for h in range(4):
                sl = slice(32 * ((q + h) % 4), 32 * ((q + h) % 4) + 32)
                kpt[h, sl, :] = kt[sl]

        @pl.when(core == 1)
        def _():
            rows = cols[:, q // 2 * 16 : q // 2 * 16 + 16, :].astype(F32)
            k = project(rows[:, q % 2 * 8 : q % 2 * 8 + 8, :].reshape(N, C).astype(BF))
            for h in range(4):
                sl = slice(32 * ((q + h) % 4), 32 * ((q + h) % 4) + 32)
                kp[h, :, sl] = k[:, sl]

    def rows_ready():
        @pl.when(core == 0)
        def _():
            rows_copy.wait_recv()

    start(0, "U", 0)
    start(0, "U", 1, 3)
    picked_send()
    arrive("U", 0)
    start_all("V", 0)
    arrive("U", 1, 3)
    start_all("V", 1, 3)
    rows_ready()
    arrive("V", 0)
    start_all("A", 0)
    arrive("V", 1, 3)
    start_all("A", 1)
    picked_end()
    line(0)
    line(1)
    line(2)
    line(3)
    arrive("A", 0)
    start(0, "B", 0)
    start_all("A", 2)
    arrive("A", 1)
    start(0, "B", 1)
    arrive("B", 0)

    lane = lax.broadcasted_iota(jnp.int32, (128, 128), 1)
    sub = lax.broadcasted_iota(jnp.int32, (128, 128), 0)
    slot = lane // 32
    slot2 = lax.broadcasted_iota(jnp.int32, (256, 128), 1) // 32

    def scores(c, p, S, M):
        for part in range(2):
            half = pl.ds(512 * part, 512)
            scores_of(c, p // 4, lax.rem(p, 4) * 2 + part, S.at[half], M.at[half])

    def scores_of(c, h, jb, S, M):
        rows = pl.ds(pl.multiple_of(jb * 128, 128), 128)
        eye = (lane == sub).astype(F32).astype(BF)
        lhs = []
        for q in range(4):
            m = (slot == lax.rem(q + h, 4)).astype(F32).astype(BF)
            lhs.append(jnp.concatenate([qr[q, rows, :] * m, eye], 1))
        lhs = jnp.concatenate(lhs, 0)
        top = None
        for n in range(4):
            if c == 0:
                b = jnp.concatenate(
                    [
                        G[jb // 2, pl.ds(lax.rem(jb, 2) * 2, 2), :, tile_at(h, lt)].reshape(128, 128)
                        for lt in (2 * n, 2 * n + 1)
                    ],
                    1,
                )
                rhs = jnp.concatenate([kpt[h, :, n * 256 : (n + 1) * 256], b], 0)
                s = jnp.dot(lhs, rhs, preferred_element_type=F32)
            else:
                b = G[n, :, :, tile_at(h, jb)].reshape(256, 128)
                rhs = jnp.concatenate([kp[h, n * 256 : (n + 1) * 256, :], b], 1)
                s = lax.dot_general(lhs, rhs, NT, preferred_element_type=F32)
            S[:, n * 256 : (n + 1) * 256] = s
            t = jnp.maximum(s[:, :128], s[:, 128:])
            top = t if top is None else jnp.maximum(top, t)
        M[...] = jnp.broadcast_to(jnp.max(top, -1, keepdims=True), (512, 128))

    def mix(p, S, M):
        h, rows = p // 4, pl.ds(pl.multiple_of(lax.rem(p, 4) * 256, 256), 256)
        weights = jnp.exp(S[...] - jnp.concatenate([M[...]] * 8, 1)).astype(BF)
        o = jnp.dot(weights, vp[h], preferred_element_type=F32)
        for q in range(4):
            oq = jnp.concatenate([o[q * 128 : (q + 1) * 128], o[512 + q * 128 : 640 + q * 128]], 0)
            val = oq[:, :128] / oq[:, 128:] * gate[q, rows, :]
            acc[q, rows, :] = jnp.where(slot2 == lax.rem(q + h, 4), val, acc[q, rows, :])

    def finish(c, p):
        rows = pl.ds(pl.multiple_of(lax.rem(p, 4) * 256, 256), 256)
        for q in range(4):
            o = jnp.dot(acc[q, rows, :].astype(BF), wo[q], preferred_element_type=F32)
            ost[q, rows, :] = (o + out_bias[c : c + 1]).astype(BF)
        out = (out0, out1)[c].at[:, rows]
        remote(ost.at[pl.ds(2 - 2 * c, 2), rows], out, ms_s.at[2 + c], ms_r.at[2 + c], partner).start()
        pltpu.make_async_copy(ost.at[pl.ds(2 * c, 2), rows], out, ms_s.at[4]).start()

    for c in range(2):
        pl.when(core == c)(lambda c=c: scores(c, 0, sA, mA))

    def event0():
        start_all("A", 3)

    def event2():
        arrive("A", 2)
        start(0, "B", 2)

    def event3():
        arrive("B", 1)

    def event6():
        arrive("A", 3)
        start(0, "B", 3)

    def event7():
        arrive("B", 2)

    def event11():
        arrive("B", 3)

    events = {0: event0, 2: event2, 3: event3, 6: event6, 7: event7, 11: event11}

    def pairs(i, _):
        for odd in range(2):
            p = 2 * i + odd
            for when, event in events.items():
                if when % 2 == odd:
                    pl.when(i == when // 2)(event)
            now, later = ((sA, mA), (sB, mB))[:: 1 - 2 * odd]
            for c in range(2):

                @pl.when(core == c)
                def _(c=c, p=p, now=now, later=later):
                    scores(c, lax.rem(p + 1, 16), *later)
                    mix(p, *now)
                    pl.when(i >= 6)(lambda: finish(c, p))

        return 0

    lax.fori_loop(0, 8, pairs, 0)

    for c, out in ((0, out0), (1, out1)):

        @pl.when(core == c)
        def _(c=c, out=out):
            pltpu.make_async_copy(ost.at[pl.ds(2 * c, 2)], out, ms_s.at[4]).wait()
            remote(ost.at[pl.ds(2 - 2 * c, 2)], out, ms_s.at[2 + c], ms_r.at[2 + c], partner).wait_send()

    for c, out in ((1, out0), (0, out1)):

        @pl.when(core == c)
        def _(c=c, out=out):
            remote(ost.at[pl.ds(0, 2)], out, ms_s.at[3 - c], ms_r.at[3 - c], partner).wait_recv()

    half_copy.wait_send()

    @pl.when(core == 0)
    def _():
        remote(pk, pk, aa_s, aa_r, partner).wait_send()

    @pl.when(core == 1)
    def _():
        most = pk.at[pl.ds(0, 63)]
        remote(most, most, aa_s, aa_r, partner).wait_send()
        rows_copy.wait_send()

    for what in (
        ("U", 0), ("U", 1, 3), ("V", 0), ("V", 1, 3), ("A", 0), ("A", 1), ("B", 0), ("A", 2), ("B", 1), ("A", 3), ("B", 2), ("B", 3)
    ):
        left(*what)


def hand_over(a, b, out0, out1, held, sems):
    parts = [(i, src.at[w], held.at[2 * i + w], dst.at[w]) for i, (src, dst) in enumerate(((a, out0), (b, out1))) for w in range(2)]
    reads = [pltpu.make_async_copy(src, mid, sems.at[0, n]) for n, (_, src, mid, _) in enumerate(parts)]
    writes = [pltpu.make_async_copy(mid, dst, sems.at[1, n]) for n, (_, _, mid, dst) in enumerate(parts)]
    for read in reads:
        read.start()
    for read, write in zip(reads, writes):
        read.wait()
        write.start()
    for write in writes:
        write.wait()


def local(pair, residue_mask, ln_gain, ln_shift, w_proj, w_bias, gate_bias, w_out, out_bias):
    vmem = pl.BlockSpec(memory_space=pltpu.VMEM)
    out = jax.ShapeDtypeStruct((2, N, C), BF)
    V = pltpu.VMEM
    dma = pltpu.SemaphoreType.DMA
    anywhere = pl.BlockSpec(memory_space=pl.ANY)
    raw = pl.pallas_call(
        body,
        out_shape=(out, out),
        in_specs=[anywhere] + [vmem] * 8,
        out_specs=(anywhere,) * 2,
        scratch_shapes=[
            V((4, 4, 4, 36, 16, 128), BF), V((RD, N, C), BF), V((N, C), F32), V((2048, C), F32), V((64, 32, C), BF),
            V((128, 32, C), BF),
            V((2, N, C), BF), V((64, N), F32), V((32, N), F32),
            V((4, 128, 512), BF), V((4, 128, 128), BF), V((4, 8, 128), F32),
            V((4, N, C), BF), V((4, N, C), BF), V((4, C, N), BF), V((4, N, 256), BF), V((4, N, C), F32), V((4, N, C), F32),
            V((1024, N), F32), V((1024, N), F32), V((1024, 128), F32), V((1024, 128), F32), V((4, N, C), BF),
            dma((120,)), dma((120,)), dma, dma, dma((5,)), dma((4,)), dma((8,)),
        ],
        compiler_params=pltpu.CompilerParams(
            collective_id=0, has_side_effects=True, vmem_limit_bytes=56 * 2**20
        ),
        cost_estimate=pl.CostEstimate(flops=20 * 10**9, bytes_accessed=4 * 2**20, transcendentals=17 * 10**6),
    )(pair, residue_mask.reshape(1, N), ln_gain, ln_shift, w_proj, jnp.transpose(w_bias, (0, 2, 1)), gate_bias, w_out, out_bias)
    return pl.pallas_call(
        hand_over, out_shape=(out, out), in_specs=[anywhere] * 2, out_specs=(anywhere,) * 2,
        scratch_shapes=[V((4, N, C), BF), dma((2, 4))],
    )(*raw)


def solution(mesh):
    return jax.shard_map(
        local,
        mesh=mesh,
        in_specs=(P(("row", "col"), None, None), P(), P(), P(), P(), P(), P(), P(), P()),
        out_specs=(P(("row", "col"), None, None), P(("row", "col"), None, None)),
        check_vma=False,
    )
```
